32 devices in a mesh: groups: 2 (over x), row: 16 (over z, y, core).
Axes of the slice: x: 2, y: 2, z: 4, core: 2. Of those that a mesh axis runs over, the one named last changes fastest.
Arguments:
- positions: float32 [8, 512, 2048], P(None, ('groups', 'row')), parts along dimension 1, may hold values from -3 to 3
- momenta: float32 [8, 512, 2048], P(None, ('groups', 'row')), parts along dimension 1, may hold values from -5 to 5
- step_size: float32 [16], P('groups'), parts along dimension 0, may hold values from 0.1 to 0.3
- counts: float32 [512, 2048], P(('groups', 'row')), parts along dimension 0, may hold values from 0 to 3
- exposure: float32 [512, 2048], P(('groups', 'row')), parts along dimension 0, may hold values from 0.05 to 0.5
- precision_diag: float32 [512, 2048], P(('groups', 'row')), parts along dimension 0, may hold values from 0.5 to 4
- kind_blocks: float32 [4, 128, 128], replicated, as said below
- vertical_coupling: float32 [128, 128], replicated, may hold values from -0.5 to 0.5
- matched_coupling: float32 [128, 128], replicated, as said below
- partner: int32 [8192], P(('groups', 'row')), parts along dimension 0, may hold values from 0 to 4095, as said below
- block_kind: int32 [512, 16], P(('groups', 'row')), parts along dimension 0, may hold values from 0 to 3
Outputs:
- new_positions: float32 [8, 512, 2048], P(None, ('groups', 'row')), parts along dimension 1
- new_momenta: float32 [8, 512, 2048], P(None, ('groups', 'row')), parts along dimension 1
The draws below stay inside these ranges and needn't reach their ends.
There are 2 independent parts, one for each index of `groups`. The reference program is written for one: setup_inputs(seed, part) draws one part's arguments, and reference() takes and returns one part's arrays. A program takes and returns all parts, laid end to end along the dimension named above; an argument that names none is the same for every part. Nothing has to cross between parts.
Inputs may be any that keep to these rules, and one draw needn't show every extreme that they name: partner pairs the blocks: partner[partner[b]] = b and partner[b] != b; the 256 blocks of each index of row have exactly 16 partners among the blocks of every index of row, their own included. `kind_blocks`: each matrix is symmetric. `matched_coupling`: symmetric.
All inputs are finite; a program needn't handle non-finite values.
Results may differ from the reference program's by a relative error of at most 0.0001.
Values sent between devices are 32-bit elements; how exact they have to be, the bound alone decides.
A program may use at most 64 MiB of HBM per device.

```python
import math
import jax
import jax.numpy as jnp
from jax import lax

CHAINS = 8
COLS = 2048
BLOCK = 128
KINDS = 4
BLOCKS_ROW = 16
BLK_DEV = 256
PAIRS = 16
GRID_ROWS = 256
BLOCKS = 4096


def symmetric_draw(key, leading, scale):
    raw_draw = jax.random.normal(key, (leading, BLOCK, BLOCK), jnp.float32)
    return (raw_draw + jnp.swapaxes(raw_draw, 1, 2)) * (scale / math.sqrt(BLOCK))


def draw_kind_blocks(key, part):
    symmetric = symmetric_draw(jax.random.fold_in(key, 11), KINDS, 0.5)
    diag_vals = jax.random.uniform(jax.random.fold_in(key, 12), (KINDS, BLOCK, 1), jnp.float32, 1.5, 3.0)
    identity = (jnp.arange(BLOCK)[:, None] == jnp.arange(BLOCK)[None, :]).astype(jnp.float32)
    return symmetric + identity[None] * diag_vals


def draw_matched_coupling(key, part):
    return symmetric_draw(jax.random.fold_in(key, 21), 1, 0.5)[0]


def draw_partner(key, part):
    devices = BLOCKS // BLK_DEV
    dev_keys = jax.random.split(jax.random.fold_in(key, 31), devices)
    orders = jax.vmap(lambda one_key: jax.random.permutation(one_key, BLK_DEV))(dev_keys).astype(jnp.int32)
    device_ids = jnp.broadcast_to(jnp.arange(devices, dtype=jnp.int32)[:, None], (devices, BLK_DEV))
    slots = jnp.broadcast_to(jnp.arange(BLK_DEV, dtype=jnp.int32)[None, :], (devices, BLK_DEV))
    target = slots // PAIRS
    offset = slots % PAIRS
    other_slot = jnp.where(target == device_ids, device_ids * PAIRS + (offset ^ 1), device_ids * PAIRS + offset)
    partner_local = orders[target, other_slot]
    partner_global = target * BLK_DEV + partner_local
    placed = jnp.zeros((devices, BLK_DEV), jnp.int32).at[device_ids, orders].set(partner_global)
    return placed.reshape(BLOCKS)


def touch_ends(entries, stream_key, least, high):
    longest = entries.shape.index(max(entries.shape))
    spots = []
    for shift in (0, 1):
        where = [jax.random.randint(jax.random.fold_in(stream_key, axis), (), 0, length) for axis, length in enumerate(entries.shape)]
        where[longest] = (where[longest] + shift) % entries.shape[longest]
        spots.append(tuple(where))
    return entries.at[spots[0]].set(least).at[spots[1]].set(high)


def steps_of(key, dims, cuts, smallest, high):
    loudness = 1.0
    for dim, blocks in cuts:
        steps = jax.random.uniform(jax.random.fold_in(jax.random.fold_in(key, 6), dim), (blocks,), jnp.float32, smallest / len(cuts), high / len(cuts))
        loudness = loudness * jnp.repeat(jnp.exp(steps), dims[dim] // blocks).reshape((-1,) + (1,) * (len(dims) - 1 - dim))
    return loudness


def centred(rng, shape, scale, most, pieces=(), kind=jnp.bfloat16):
    loudness = steps_of(rng, shape, pieces, -0.22, 0.18) if pieces else 1.0
    array = jax.random.normal(rng, shape, jnp.float32) * scale * loudness
    return jnp.minimum(jnp.maximum(array, -most), most).astype(kind)


def setup_inputs(seed: int = 0, part: int = 0) -> dict:
    key_list = jax.random.split(jax.random.key(seed), 12)
    part_keys = jax.random.split(jax.random.fold_in(key_list[11], part), 12)
    positions = centred(part_keys[0], (CHAINS, GRID_ROWS, COLS), 0.5, 3.0, ((1, 16),), jnp.float32)
    momenta = centred(part_keys[1], (CHAINS, GRID_ROWS, COLS), 1.0, 5.0, ((1, 16),), jnp.float32)
    step_size = jnp.clip(jnp.exp(jax.random.uniform(part_keys[2], (CHAINS,), jnp.float32, math.log(0.1), math.log(0.3))), 0.1, 0.3)
    counts = jnp.clip(3.0 * jax.random.uniform(part_keys[3], (GRID_ROWS, COLS), jnp.float32) ** steps_of(part_keys[3], (GRID_ROWS, COLS), ((0, 16),), -0.2, 0.2), 0.0, 3.0)
    exposure = jnp.clip(jnp.exp(math.log(0.5) - 2.3025851 * jax.random.uniform(part_keys[4], (GRID_ROWS, COLS), jnp.float32) ** steps_of(part_keys[4], (GRID_ROWS, COLS), ((0, 16),), -0.2, 0.2)), 0.05, 0.5)
    precision_diag = jnp.clip(jnp.exp(math.log(4.0) - 2.0794415 * jax.random.uniform(part_keys[5], (GRID_ROWS, COLS), jnp.float32) ** steps_of(part_keys[5], (GRID_ROWS, COLS), ((0, 16),), -0.2, 0.2)), 0.5, 4.0)
    kind_blocks = draw_kind_blocks(jax.random.fold_in(key_list[11], 71), part)
    vertical_coupling = centred(key_list[7], (BLOCK, BLOCK), BLOCK ** -0.5, 0.5, (), jnp.float32)
    matched_coupling = draw_matched_coupling(jax.random.fold_in(key_list[11], 71), part)
    partner = draw_partner(jax.random.fold_in(jax.random.fold_in(key_list[11], part), 71), part)
    block_kind = touch_ends(jax.random.randint(part_keys[10], (GRID_ROWS, BLOCKS_ROW), 0, KINDS), jax.random.fold_in(part_keys[10], 1), 0, KINDS - 1).astype(jnp.int32)
    return {"positions": positions, "momenta": momenta, "step_size": step_size, "counts": counts, "exposure": exposure, "precision_diag": precision_diag, "kind_blocks": kind_blocks, "vertical_coupling": vertical_coupling, "matched_coupling": matched_coupling, "partner": partner, "block_kind": block_kind}


highest = lax.Precision.HIGHEST

def potential_grad(current, counts, exposure, precision_diag, kind_blocks, vertical_coupling, matched_coupling, partner, block_kind):
    chains, grid_rows, grid_cols = current.shape
    block_width = kind_blocks.shape[1]
    per_row = grid_cols // block_width
    blocks = current.reshape(chains, grid_rows, per_row, block_width)
    within = jnp.zeros(blocks.shape, jnp.float32)
    for kind_id in range(kind_blocks.shape[0]):
        product = jnp.einsum('crnk,kl->crnl', blocks, kind_blocks[kind_id], precision=highest)
        within = within + jnp.where((block_kind == kind_id)[None, :, :, None], product, jnp.zeros_like(product))
    zero_row = jnp.zeros((chains, 1, per_row, block_width), current.dtype)
    lower_rows = jnp.concatenate([blocks[:, 1:], zero_row], axis=1)
    upper_rows = jnp.concatenate([zero_row, blocks[:, :-1]], axis=1)
    vertical = jnp.einsum('crnk,lk->crnl', lower_rows, vertical_coupling, precision=highest)
    vertical = vertical + jnp.einsum('crnk,kl->crnl', upper_rows, vertical_coupling, precision=highest)
    flat_blocks = blocks.reshape(chains, grid_rows * per_row, block_width)
    partner_vals = jnp.take(flat_blocks, partner.astype(jnp.int32), axis=1)
    matched = jnp.einsum('cbk,kl->cbl', partner_vals, matched_coupling, precision=highest)
    matched = matched.reshape(chains, grid_rows, per_row, block_width)
    coupled = (within - vertical - matched).reshape(chains, grid_rows, grid_cols)
    return coupled + precision_diag[None] * current - counts[None] + exposure[None] * jnp.exp(current)

def reference(positions, momenta, step_size, counts, exposure, precision_diag, kind_blocks, vertical_coupling, matched_coupling, partner, block_kind):
    step_len = step_size[:, None, None]

    def gradient_at(current):
        return potential_grad(current, counts, exposure, precision_diag, kind_blocks, vertical_coupling, matched_coupling, partner, block_kind)
    half_step = momenta - 0.5 * step_len * gradient_at(positions)
    moved_once = positions + step_len * half_step
    full_step = half_step - step_len * gradient_at(moved_once)
    new_positions = moved_once + step_len * full_step
    new_momenta = full_step - 0.5 * step_len * gradient_at(new_positions)
    return (new_positions, new_momenta)
```

```python
import functools

import jax
import jax.numpy as jnp
from jax import lax
from jax.experimental import pallas as pl
from jax.experimental.pallas import tpu as pltpu
from jax.sharding import PartitionSpec as P

MESH = pl.DeviceIdType.MESH
bf16 = jnp.bfloat16
f32 = jnp.float32


def split(value):
    high = value.astype(bf16)
    low = (value - high.astype(f32)).astype(bf16)
    return high, low


def dot(a, b):
    return jnp.dot(a, b, preferred_element_type=f32)


def kernel(
    n,
    order_ref,
    pos_ref,
    x_ref,
    p_ref,
    step_ref,
    counts_ref,
    exposure_ref,
    diag_ref,
    kind_ref,
    kb_ref,
    vert_ref,
    match_ref,
    newx_ref,
    newp_ref,
    half_ref,
    w_ref,
    moved_ref,
    wfull_ref,
    w2_ref,
    q1_ref,
    q2_ref,
    vh_ref,
    vl_ref,
    kh_ref,
    kl_ref,
    uh_ref,
    ul_ref,
    mh_ref,
    ml_ref,
    send0,
    send1,
    send2,
    recv0,
    recv1,
    recv2,
    halo0,
    halo1,
    halo2,
    send_sem,
    recv_sem,
    edge_send,
    edge_recv,
):
    me = lax.axis_index("row")
    blocks, chains, width = x_ref.shape
    kinds = kb_ref.shape[0]
    per = 16
    rows = blocks // per
    lines = per * chains
    pairs = blocks // n
    sends = (send0, send1, send2)
    recvs = (recv0, recv1, recv2)
    halos = (halo0, halo1, halo2)

    barrier = pltpu.get_barrier_semaphore()

    @pl.loop(1, n)
    def _(d):
        pl.semaphore_signal(
            barrier, inc=1, device_id={"row": lax.rem(me + d, n)}, device_id_type=MESH
        )

    pl.semaphore_wait(barrier, n - 1)

    def edge_copy(src, phase, down):
        where = blocks - per if down else 0
        side = 0 if down else 1
        peer = lax.rem(me + (1 if down else n - 1), n)
        return pltpu.make_async_remote_copy(
            src_ref=src.at[pl.ds(where, per)],
            dst_ref=halos[phase].at[side],
            send_sem=edge_send.at[phase, side],
            recv_sem=edge_recv.at[phase, side],
            device_id={"row": peer},
            device_id_type=MESH,
        )

    def start_edges(src, phase):
        @pl.when(me < n - 1)
        def _():
            edge_copy(src, phase, True).start()

        @pl.when(me > 0)
        def _():
            edge_copy(src, phase, False).start()

    def wait_edges(src, phase):
        @pl.when(me > 0)
        def _():
            edge_copy(src, phase, True).wait_recv()

        @pl.when(me < n - 1)
        def _():
            edge_copy(src, phase, False).wait_recv()

    def drain_edges(src, phase):
        @pl.when(me < n - 1)
        def _():
            edge_copy(src, phase, True).wait_send()

        @pl.when(me > 0)
        def _():
            edge_copy(src, phase, False).wait_send()

    def slab_copy(phase, peer, here, there):
        return pltpu.make_async_remote_copy(
            src_ref=sends[phase].at[pl.ds(peer * pairs, pairs)],
            dst_ref=recvs[phase].at[pl.ds(here * pairs, pairs)],
            send_sem=send_sem.at[phase, peer],
            recv_sem=recv_sem.at[phase, there],
            device_id={"row": peer},
            device_id_type=MESH,
        )

    def start_exchange(src, phase):
        @pl.loop(0, n - 1)
        def _(k):
            peer = lax.rem(me + 1 + lax.rem(n // 2 - 1 + k, n - 1), n)
            for i in range(pairs):
                sends[phase][peer * pairs + i] = src[order_ref[peer * pairs + i]]
            slab_copy(phase, peer, me, me).start()

        for i in range(pairs):
            recvs[phase][me * pairs + i] = src[order_ref[me * pairs + i]]

    def wait_exchange(phase):
        @pl.loop(1, n)
        def _(d):
            peer = lax.rem(me + d, n)
            slab_copy(phase, peer, me, peer).wait_recv()

    def drain_exchange(phase):
        @pl.loop(1, n)
        def _(d):
            peer = lax.rem(me + d, n)
            slab_copy(phase, peer, me, me).wait_send()

    start_edges(x_ref, 0)
    start_exchange(x_ref, 0)

    for q in range(kinds):
        high, low = split(kb_ref[q])
        kh_ref[:width, q * width : (q + 1) * width] = high
        kh_ref[width:, q * width : (q + 1) * width] = high
        kl_ref[:, q * width : (q + 1) * width] = low
    high, low = split(vert_ref[...].T)
    uh_ref[:width] = high
    ul_ref[:width] = low
    high, low = split(vert_ref[...])
    uh_ref[width:] = high
    ul_ref[width:] = low
    high, low = split(match_ref[...])
    mh_ref[:width] = high
    mh_ref[width:] = high
    ml_ref[...] = low

    step = step_ref[...][None]
    tile = (per, chains, width)

    def times_match(value):
        high, low = split(value)
        both = jnp.concatenate([high, low], axis=1)
        return dot(both, mh_ref[...]) + dot(high, ml_ref[...])

    def fill(src):
        @pl.loop(0, rows)
        def _(r):
            high, low = split(src[pl.ds(r * per, per)].reshape(lines, width))
            vh_ref[pl.ds((r + 1) * lines, lines)] = high
            vl_ref[pl.ds((r + 1) * lines, lines)] = low

    def fill_halo(phase):
        for side, outside in ((0, me == 0), (1, me == n - 1)):
            value = halos[phase][side].reshape(lines, width)
            value = jnp.where(outside, jnp.zeros_like(value), value)
            high, low = split(value)
            at = side * (rows + 1) * lines
            vh_ref[at : at + lines] = high
            vl_ref[at : at + lines] = low

    def local_grad(src, r):
        here = pl.ds(r * per, per)
        vh = vh_ref[pl.ds((r + 1) * lines, lines)]
        vl = vl_ref[pl.ds((r + 1) * lines, lines)]
        within = dot(jnp.concatenate([vh, vl], axis=1), kh_ref[...]) + dot(vh, kl_ref[...])
        kind = jnp.broadcast_to(kind_ref[here], tile)
        own = within[:, :width].reshape(tile)
        for q in range(1, kinds):
            own = jnp.where(kind == q, within[:, q * width : (q + 1) * width].reshape(tile), own)
        above, below = pl.ds(r * lines, lines), pl.ds((r + 2) * lines, lines)
        sh = jnp.concatenate([vh_ref[below], vh_ref[above]], axis=1)
        sl = jnp.concatenate([vl_ref[below], vl_ref[above]], axis=1)
        vertical = dot(sh, uh_ref[...]) + dot(sl, uh_ref[...]) + dot(sh, ul_ref[...])
        value = src[here]
        return (
            own
            - vertical.reshape(tile)
            + diag_ref[here] * value
            - counts_ref[here]
            + exposure_ref[here] * jnp.exp(value)
        )

    def all_rows(src, phase, use):
        fill(src)

        @pl.loop(1, rows - 1)
        def _(r):
            use(r, local_grad(src, r))

        wait_edges(src, phase)
        fill_halo(phase)

        @pl.loop(0, 2)
        def _(e):
            r = e * (rows - 1)
            use(r, local_grad(src, r))

    def received(phase, r):
        return jnp.concatenate(
            [recvs[phase][pos_ref[r * per + i]] for i in range(per)], axis=0
        )

    def use_first(r, grad):
        here = pl.ds(r * per, per)
        half = p_ref[here] - 0.5 * step * grad
        half_ref[here] = half
        w_ref[here] = x_ref[here] + step * half

    all_rows(x_ref, 0, use_first)
    start_exchange(w_ref, 1)

    @pl.loop(0, rows)
    def _(r):
        here = pl.ds(r * per, per)
        product = times_match(x_ref[here].reshape(lines, width)).reshape(tile)
        q1_ref[here] = 0.5 * step * step * product

    wait_exchange(0)

    @pl.loop(0, rows)
    def _(r):
        here = pl.ds(r * per, per)
        matched = times_match(received(0, r)).reshape(tile)
        half_ref[here] = half_ref[here] + 0.5 * step * matched
        moved_ref[here] = w_ref[here] + 0.5 * step * step * matched

    start_edges(moved_ref, 1)

    def use_second(r, grad):
        here = pl.ds(r * per, per)
        full = half_ref[here] - step * grad
        wfull_ref[here] = full
        w2_ref[here] = moved_ref[here] + step * full

    all_rows(moved_ref, 1, use_second)
    start_exchange(w2_ref, 2)

    @pl.loop(0, rows)
    def _(r):
        here = pl.ds(r * per, per)
        product = times_match(moved_ref[here].reshape(lines, width)).reshape(tile)
        q2_ref[here] = step * step * product

    wait_exchange(1)

    @pl.loop(0, rows)
    def _(r):
        here = pl.ds(r * per, per)
        value = received(1, r) + q1_ref[here].reshape(lines, width)
        matched = times_match(value).reshape(tile)
        wfull_ref[here] = wfull_ref[here] + step * matched
        newx_ref[here] = w2_ref[here] + step * step * matched

    start_edges(newx_ref, 2)

    def use_third(r, grad):
        here = pl.ds(r * per, per)
        newp_ref[here] = wfull_ref[here] - 0.5 * step * grad

    all_rows(newx_ref, 2, use_third)
    wait_exchange(2)

    @pl.loop(0, rows)
    def _(r):
        here = pl.ds(r * per, per)
        value = received(2, r) + q2_ref[here].reshape(lines, width)
        matched = times_match(value).reshape(tile)
        newp_ref[here] = newp_ref[here] + 0.5 * step * matched

    for phase, src in enumerate((x_ref, moved_ref, newx_ref)):
        drain_edges(src, phase)
        drain_exchange(phase)


def body(
    positions,
    momenta,
    step_size,
    counts,
    exposure,
    precision_diag,
    kind_blocks,
    vertical_coupling,
    matched_coupling,
    partner,
    block_kind,
):
    n = lax.axis_size("row")
    chains, rows, cols = positions.shape
    kinds, width = kind_blocks.shape[:2]
    per = cols // width
    blocks = rows * per

    ids = jnp.arange(blocks, dtype=jnp.int32)
    key = (partner // blocks) * blocks + ids
    slot = jnp.sum((key[None, :] < key[:, None]).astype(jnp.int32), axis=1)
    pos = jnp.sum((partner[None, :] < partner[:, None]).astype(jnp.int32), axis=1)
    order = jnp.sum(jnp.where(slot[None, :] == ids[:, None], ids[None, :], 0), axis=1)

    def to_blocks(v):
        return v.reshape(chains, rows, per, width).transpose(1, 2, 0, 3).reshape(
            blocks, chains, width
        )

    def from_blocks(v):
        return v.reshape(rows, per, chains, width).transpose(2, 0, 1, 3).reshape(
            chains, rows, cols
        )

    def unit(v):
        return v.reshape(blocks, 1, width)

    kind = jnp.broadcast_to(block_kind.reshape(blocks, 1, 1), (blocks, 1, width))
    step = jnp.broadcast_to(step_size[:, None], (chains, width))
    vmem = pl.BlockSpec(memory_space=pltpu.VMEM)
    smem = pl.BlockSpec(memory_space=pltpu.SMEM)
    field = (blocks, chains, width)
    lines = per * chains
    big = lambda: pltpu.VMEM(field, f32)
    newx, newp = pl.pallas_call(
        functools.partial(kernel, n),
        out_shape=(jax.ShapeDtypeStruct(field, f32), jax.ShapeDtypeStruct(field, f32)),
        in_specs=[smem] * 2 + [vmem] * 10,
        out_specs=(vmem, vmem),
        scratch_shapes=[big() for _ in range(7)]
        + [
            pltpu.VMEM(((rows + 2) * lines, width), bf16),
            pltpu.VMEM(((rows + 2) * lines, width), bf16),
            pltpu.VMEM((2 * width, kinds * width), bf16),
            pltpu.VMEM((width, kinds * width), bf16),
            pltpu.VMEM((2 * width, width), bf16),
            pltpu.VMEM((2 * width, width), bf16),
            pltpu.VMEM((2 * width, width), bf16),
            pltpu.VMEM((width, width), bf16),
        ]
        + [big() for _ in range(6)]
        + [pltpu.VMEM((2, per, chains, width), f32) for _ in range(3)]
        + [
            pltpu.SemaphoreType.DMA((3, n)),
            pltpu.SemaphoreType.DMA((3, n)),
            pltpu.SemaphoreType.DMA((3, 2)),
            pltpu.SemaphoreType.DMA((3, 2)),
        ],
        compiler_params=pltpu.CompilerParams(
            collective_id=0, has_side_effects=True, vmem_limit_bytes=48 * 1024 * 1024
        ),
    )(
        order,
        pos,
        to_blocks(positions),
        to_blocks(momenta),
        step,
        unit(counts),
        unit(exposure),
        unit(precision_diag),
        kind,
        kind_blocks,
        vertical_coupling,
        matched_coupling,
    )
    return from_blocks(newx), from_blocks(newp)


def solution(mesh):
    return jax.shard_map(
        body,
        mesh=mesh,
        in_specs=(
            P(None, ("groups", "row"), None),
            P(None, ("groups", "row"), None),
            P("groups"),
            P(("groups", "row"), None),
            P(("groups", "row"), None),
            P(("groups", "row"), None),
            P(),
            P(),
            P(),
            P(("groups", "row")),
            P(("groups", "row"), None),
        ),
        out_specs=(P(None, ("groups", "row"), None), P(None, ("groups", "row"), None)),
        check_vma=False,
    )
```

```python
import functools

import jax
import jax.numpy as jnp
from jax import lax
from jax.experimental import pallas as pl
from jax.experimental.pallas import tpu as pltpu
from jax.sharding import PartitionSpec as P

MESH = pl.DeviceIdType.MESH
bf16 = jnp.bfloat16
f32 = jnp.float32


def split(value):
    high = value.astype(bf16)
    low = (value - high.astype(f32)).astype(bf16)
    return high, low


def dot(a, b):
    return jnp.dot(a, b, preferred_element_type=f32)


def kernel(
    n,
    order_ref,
    pos_ref,
    step_ref,
    kind_ref,
    xin_ref,
    pin_ref,
    counts_in,
    exposure_in,
    diag_in,
    kb_in,
    vert_in,
    match_in,
    xout_ref,
    pout_ref,
    x_ref,
    newx_ref,
    newp_ref,
    half_ref,
    w_ref,
    moved_ref,
    wfull_ref,
    w2_ref,
    q1_ref,
    q2_ref,
    vh_ref,
    vl_ref,
    kh_ref,
    kl_ref,
    uh_ref,
    ul_ref,
    mh_ref,
    ml_ref,
    send0,
    send1,
    send2,
    recv0,
    recv1,
    recv2,
    halo0,
    halo1,
    halo2,
    send_sem,
    recv_sem,
    edge_send,
    edge_recv,
    xheld,
    pheld,
    xoheld,
    poheld,
    local_sem,
    counts_ref,
    exposure_ref,
    diag_ref,
    kb_ref,
    vert_ref,
    match_ref,
    small_sem,
):
    me = lax.axis_index("row")
    blocks, chains, width = x_ref.shape
    kinds = kb_ref.shape[0]
    rows, per = kind_ref.shape
    lines = per * chains
    pairs = blocks // n
    sends = (send0, send1, send2)
    recvs = (recv0, recv1, recv2)
    halos = (halo0, halo1, halo2)

    barrier = pltpu.get_barrier_semaphore()

    @pl.loop(0, per)
    def _(j):
        pltpu.make_async_copy(
            xin_ref.at[:, pl.ds(pl.multiple_of(j * width, width), width)],
            xheld.at[j],
            local_sem.at[0, j],
        ).start()

    @pl.loop(1, n)
    def _(d):
        pl.semaphore_signal(
            barrier, inc=1, device_id={"row": lax.rem(me + d, n)}, device_id_type=MESH
        )

    def panel(whole, held, which, j, out=False):
        far, near = whole.at[:, pl.ds(pl.multiple_of(j * width, width), width)], held.at[j]
        if out:
            far, near = near, far
        return pltpu.make_async_copy(far, near, local_sem.at[which, j])

    def take_row(held, r):
        return jnp.stack([held[j, pl.ds(r, chains, stride=rows), :] for j in range(per)])

    def put_row(held, r, value):
        for j in range(per):
            held[j, pl.ds(r, chains, stride=rows), :] = value[j]

    def start_panels(whole, held, which, out=False):
        @pl.loop(0, per)
        def _(j):
            panel(whole, held, which, j, out).start()

    def wait_panels(whole, held, which, out=False):
        @pl.loop(0, per)
        def _(j):
            panel(whole, held, which, j, out).wait()

    @pl.loop(0, per)
    def _(j):
        panel(xin_ref, xheld, 0, j).wait()
        for r in range(rows):
            x_ref[r * per + j] = xheld[j, pl.ds(r, chains, stride=rows), :]

    small = [
        pltpu.make_async_copy(far, near, small_sem.at[i])
        for i, (far, near) in enumerate(
            (
                (kb_in, kb_ref),
                (vert_in, vert_ref),
                (match_in, match_ref),
                (counts_in, counts_ref),
                (exposure_in, exposure_ref),
                (diag_in, diag_ref),
            )
        )
    ]
    for copy in small:
        copy.start()
    start_panels(pin_ref, pheld, 1)
    pl.semaphore_wait(barrier, n - 1)

    def edge_copy(src, phase, down):
        where = blocks - per if down else 0
        side = 0 if down else 1
        peer = lax.rem(me + (1 if down else n - 1), n)
        return pltpu.make_async_remote_copy(
            src_ref=src.at[pl.ds(where, per)],
            dst_ref=halos[phase].at[side],
            send_sem=edge_send.at[phase, side],
            recv_sem=edge_recv.at[phase, side],
            device_id={"row": peer},
            device_id_type=MESH,
        )

    def start_edges(src, phase):
        @pl.when(me < n - 1)
        def _():
            edge_copy(src, phase, True).start()

        @pl.when(me > 0)
        def _():
            edge_copy(src, phase, False).start()

    def wait_edges(src, phase):
        @pl.when(me > 0)
        def _():
            edge_copy(src, phase, True).wait_recv()

        @pl.when(me < n - 1)
        def _():
            edge_copy(src, phase, False).wait_recv()

    def drain_edges(src, phase):
        @pl.when(me < n - 1)
        def _():
            edge_copy(src, phase, True).wait_send()

        @pl.when(me > 0)
        def _():
            edge_copy(src, phase, False).wait_send()

    def slab_copy(phase, peer, here, there):
        return pltpu.make_async_remote_copy(
            src_ref=sends[phase].at[pl.ds(peer * pairs, pairs)],
            dst_ref=recvs[phase].at[pl.ds(here * pairs, pairs)],
            send_sem=send_sem.at[phase, peer],
            recv_sem=recv_sem.at[phase, there],
            device_id={"row": peer},
            device_id_type=MESH,
        )

    def start_exchange(src, phase):
        @pl.loop(0, n - 1)
        def _(k):
            peer = lax.rem(me + 1 + lax.rem(n // 2 - 1 + k, n - 1), n)
            for i in range(pairs):
                sends[phase][peer * pairs + i] = src[order_ref[peer * pairs + i]]
            slab_copy(phase, peer, me, me).start()

        for i in range(pairs):
            recvs[phase][me * pairs + i] = src[order_ref[me * pairs + i]]

    def wait_exchange(phase):
        @pl.loop(1, n)
        def _(d):
            peer = lax.rem(me + d, n)
            slab_copy(phase, peer, me, peer).wait_recv()

    def drain_exchange(phase):
        @pl.loop(1, n)
        def _(d):
            peer = lax.rem(me + d, n)
            slab_copy(phase, peer, me, me).wait_send()

    start_edges(x_ref, 0)
    start_exchange(x_ref, 0)

    for copy in small:
        copy.wait()
    for q in range(kinds):
        high, low = split(kb_ref[q])
        kh_ref[:width, q * width : (q + 1) * width] = high
        kh_ref[width:, q * width : (q + 1) * width] = high
        kl_ref[:, q * width : (q + 1) * width] = low
    high, low = split(vert_ref[...].T)
    uh_ref[:width] = high
    ul_ref[:width] = low
    high, low = split(vert_ref[...])
    uh_ref[width:] = high
    ul_ref[width:] = low
    high, low = split(match_ref[...])
    mh_ref[:width] = high
    mh_ref[width:] = high
    ml_ref[...] = low

    tile = (per, chains, width)
    chain = lax.broadcasted_iota(jnp.int32, (chains, width), 0)
    step = jnp.zeros((chains, width), f32)
    for c in range(chains):
        step = jnp.where(chain == c, step_ref[c], step)
    step = step[None]

    def unit_row(src, r):
        line = src[pl.ds(r, 1), :]
        return jnp.stack(
            [
                jnp.broadcast_to(line[:, j * width : (j + 1) * width], (chains, width))
                for j in range(per)
            ]
        )

    def times_match(value):
        high, low = split(value)
        both = jnp.concatenate([high, low], axis=1)
        return dot(both, mh_ref[...]) + dot(high, ml_ref[...])

    def fill(src):
        @pl.loop(0, rows)
        def _(r):
            high, low = split(src[pl.ds(r * per, per)].reshape(lines, width))
            vh_ref[pl.ds((r + 1) * lines, lines)] = high
            vl_ref[pl.ds((r + 1) * lines, lines)] = low

    def fill_halo(phase):
        for side, outside in ((0, me == 0), (1, me == n - 1)):
            value = halos[phase][side].reshape(lines, width)
            value = jnp.where(outside, jnp.zeros_like(value), value)
            high, low = split(value)
            at = side * (rows + 1) * lines
            vh_ref[at : at + lines] = high
            vl_ref[at : at + lines] = low

    def local_grad(src, r):
        here = pl.ds(r * per, per)
        vh = vh_ref[pl.ds((r + 1) * lines, lines)]
        vl = vl_ref[pl.ds((r + 1) * lines, lines)]
        within = dot(jnp.concatenate([vh, vl], axis=1), kh_ref[...]) + dot(vh, kl_ref[...])
        kind = jnp.stack([jnp.full((chains, width), kind_ref[r, j]) for j in range(per)])
        own = within[:, :width].reshape(tile)
        for q in range(1, kinds):
            own = jnp.where(kind == q, within[:, q * width : (q + 1) * width].reshape(tile), own)
        above, below = pl.ds(r * lines, lines), pl.ds((r + 2) * lines, lines)
        sh = jnp.concatenate([vh_ref[below], vh_ref[above]], axis=1)
        sl = jnp.concatenate([vl_ref[below], vl_ref[above]], axis=1)
        vertical = dot(sh, uh_ref[...]) + dot(sl, uh_ref[...]) + dot(sh, ul_ref[...])
        value = src[here]
        return (
            own
            - vertical.reshape(tile)
            + unit_row(diag_ref, r) * value
            - unit_row(counts_ref, r)
            + unit_row(exposure_ref, r) * jnp.exp(value)
        )

    def all_rows(src, phase, use):
        fill(src)

        @pl.loop(1, rows - 1)
        def _(r):
            use(r, local_grad(src, r))

        wait_edges(src, phase)
        fill_halo(phase)

        @pl.loop(0, 2)
        def _(e):
            r = e * (rows - 1)
            use(r, local_grad(src, r))

    def received(phase, r):
        return jnp.concatenate(
            [recvs[phase][pos_ref[r * per + i]] for i in range(per)], axis=0
        )

    def use_first(r, grad):
        here = pl.ds(r * per, per)
        half = take_row(pheld, r) - 0.5 * step * grad
        half_ref[here] = half
        w_ref[here] = x_ref[here] + step * half

    wait_panels(pin_ref, pheld, 1)
    all_rows(x_ref, 0, use_first)
    start_exchange(w_ref, 1)

    @pl.loop(0, rows)
    def _(r):
        here = pl.ds(r * per, per)
        product = times_match(x_ref[here].reshape(lines, width)).reshape(tile)
        q1_ref[here] = 0.5 * step * step * product

    wait_exchange(0)

    @pl.loop(0, rows)
    def _(r):
        here = pl.ds(r * per, per)
        matched = times_match(received(0, r)).reshape(tile)
        half_ref[here] = half_ref[here] + 0.5 * step * matched
        moved_ref[here] = w_ref[here] + 0.5 * step * step * matched

    start_edges(moved_ref, 1)

    def use_second(r, grad):
        here = pl.ds(r * per, per)
        full = half_ref[here] - step * grad
        wfull_ref[here] = full
        w2_ref[here] = moved_ref[here] + step * full

    all_rows(moved_ref, 1, use_second)
    start_exchange(w2_ref, 2)

    @pl.loop(0, rows)
    def _(r):
        here = pl.ds(r * per, per)
        product = times_match(moved_ref[here].reshape(lines, width)).reshape(tile)
        q2_ref[here] = step * step * product

    wait_exchange(1)

    @pl.loop(0, rows)
    def _(r):
        here = pl.ds(r * per, per)
        value = received(1, r) + q1_ref[here].reshape(lines, width)
        matched = times_match(value).reshape(tile)
        wfull_ref[here] = wfull_ref[here] + step * matched
        newx = w2_ref[here] + step * step * matched
        newx_ref[here] = newx
        put_row(xoheld, r, newx)

    start_edges(newx_ref, 2)
    start_panels(xout_ref, xoheld, 2, True)

    def use_third(r, grad):
        here = pl.ds(r * per, per)
        newp_ref[here] = wfull_ref[here] - 0.5 * step * grad

    all_rows(newx_ref, 2, use_third)
    wait_exchange(2)

    @pl.loop(0, rows)
    def _(r):
        here = pl.ds(r * per, per)
        value = received(2, r) + q2_ref[here].reshape(lines, width)
        matched = times_match(value).reshape(tile)
        put_row(poheld, r, newp_ref[here] + 0.5 * step * matched)

    start_panels(pout_ref, poheld, 3, True)
    for phase, src in enumerate((x_ref, moved_ref, newx_ref)):
        drain_edges(src, phase)
        drain_exchange(phase)
    wait_panels(xout_ref, xoheld, 2, True)
    wait_panels(pout_ref, poheld, 3, True)


def body(
    positions,
    momenta,
    step_size,
    counts,
    exposure,
    precision_diag,
    kind_blocks,
    vertical_coupling,
    matched_coupling,
    partner,
    block_kind,
):
    n = lax.axis_size("row")
    chains, rows, cols = positions.shape
    kinds, width = kind_blocks.shape[:2]
    per = cols // width
    blocks = rows * per

    ids = jnp.arange(blocks, dtype=jnp.int32)
    key = (partner // blocks) * blocks + ids
    slot = jnp.sum((key[None, :] < key[:, None]).astype(jnp.int32), axis=1)
    pos = jnp.sum((partner[None, :] < partner[:, None]).astype(jnp.int32), axis=1)
    order = jnp.sum(jnp.where(slot[None, :] == ids[:, None], ids[None, :], 0), axis=1)

    hbm = pl.BlockSpec(memory_space=pl.ANY)
    smem = pl.BlockSpec(memory_space=pltpu.SMEM)
    field = (blocks, chains, width)
    lines = per * chains
    big = lambda: pltpu.VMEM(field, f32)
    flat = (chains * rows, cols)
    newx, newp = pl.pallas_call(
        functools.partial(kernel, n),
        out_shape=(jax.ShapeDtypeStruct(flat, f32), jax.ShapeDtypeStruct(flat, f32)),
        in_specs=[smem] * 4 + [hbm] * 8,
        out_specs=(hbm, hbm),
        scratch_shapes=[big() for _ in range(10)]
        + [
            pltpu.VMEM(((rows + 2) * lines, width), bf16),
            pltpu.VMEM(((rows + 2) * lines, width), bf16),
            pltpu.VMEM((2 * width, kinds * width), bf16),
            pltpu.VMEM((width, kinds * width), bf16),
            pltpu.VMEM((2 * width, width), bf16),
            pltpu.VMEM((2 * width, width), bf16),
            pltpu.VMEM((2 * width, width), bf16),
            pltpu.VMEM((width, width), bf16),
        ]
        + [big() for _ in range(6)]
        + [pltpu.VMEM((2, per, chains, width), f32) for _ in range(3)]
        + [
            pltpu.SemaphoreType.DMA((3, n)),
            pltpu.SemaphoreType.DMA((3, n)),
            pltpu.SemaphoreType.DMA((3, 2)),
            pltpu.SemaphoreType.DMA((3, 2)),
        ]
        + [pltpu.VMEM((per, chains * rows, width), f32) for _ in range(4)]
        + [pltpu.SemaphoreType.DMA((4, per))]
        + [pltpu.VMEM((rows, cols), f32) for _ in range(3)]
        + [
            pltpu.VMEM((kinds, width, width), f32),
            pltpu.VMEM((width, width), f32),
            pltpu.VMEM((width, width), f32),
            pltpu.SemaphoreType.DMA((6,)),
        ],
        compiler_params=pltpu.CompilerParams(
            collective_id=0, has_side_effects=True, vmem_limit_bytes=60 * 1024 * 1024
        ),
    )(
        order,
        pos,
        step_size,
        block_kind,
        positions.reshape(flat),
        momenta.reshape(flat),
        counts,
        exposure,
        precision_diag,
        kind_blocks,
        vertical_coupling,
        matched_coupling,
    )
    return newx.reshape(positions.shape), newp.reshape(positions.shape)


def solution(mesh):
    return jax.shard_map(
        body,
        mesh=mesh,
        in_specs=(
            P(None, ("groups", "row"), None),
            P(None, ("groups", "row"), None),
            P("groups"),
            P(("groups", "row"), None),
            P(("groups", "row"), None),
            P(("groups", "row"), None),
            P(),
            P(),
            P(),
            P(("groups", "row")),
            P(("groups", "row"), None),
        ),
        out_specs=(P(None, ("groups", "row"), None), P(None, ("groups", "row"), None)),
        check_vma=False,
    )
```

```python
import functools

import jax
import jax.numpy as jnp
from jax import lax
from jax.experimental import pallas as pl
from jax.experimental.pallas import tpu as pltpu
from jax.sharding import PartitionSpec as P

MESH = pl.DeviceIdType.MESH
bf16 = jnp.bfloat16
f32 = jnp.float32


def split(value):
    high = value.astype(bf16)
    low = (value - high.astype(f32)).astype(bf16)
    return high, low


def dot(a, b):
    return jnp.dot(a, b, preferred_element_type=f32)


def kernel(
    n,
    order_ref,
    pos_ref,
    step_ref,
    kind_ref,
    xin_ref,
    pin_ref,
    counts_in,
    exposure_in,
    diag_in,
    kb_in,
    vert_in,
    match_in,
    xout_ref,
    pout_ref,
    x_ref,
    newx_ref,
    newp_ref,
    half_ref,
    w_ref,
    moved_ref,
    wfull_ref,
    w2_ref,
    q1_ref,
    q2_ref,
    vh_ref,
    vl_ref,
    kh_ref,
    kl_ref,
    uh_ref,
    ul_ref,
    mh_ref,
    ml_ref,
    send0,
    send1,
    send2,
    recv0,
    recv1,
    recv2,
    halo0,
    halo1,
    halo2,
    send_sem,
    recv_sem,
    edge_send,
    edge_recv,
    xheld,
    pheld,
    xoheld,
    poheld,
    local_sem,
    counts_ref,
    exposure_ref,
    diag_ref,
    kb_ref,
    vert_ref,
    match_ref,
    small_sem,
):
    me = lax.axis_index("row")
    blocks, chains, width = x_ref.shape
    kinds = kb_ref.shape[0]
    rows, per = kind_ref.shape
    lines = per * chains
    pairs = blocks // n
    sends = (send0, send1, send2)
    recvs = (recv0, recv1, recv2)
    halos = (halo0, halo1, halo2)

    barrier = pltpu.get_barrier_semaphore()

    @pl.loop(0, per)
    def _(j):
        pltpu.make_async_copy(
            xin_ref.at[:, pl.ds(pl.multiple_of(j * width, width), width)],
            xheld.at[j],
            local_sem.at[0, j],
        ).start()

    @pl.loop(1, n)
    def _(d):
        pl.semaphore_signal(
            barrier, inc=1, device_id={"row": lax.rem(me + d, n)}, device_id_type=MESH
        )

    def panel(whole, held, which, j, out=False):
        far, near = whole.at[:, pl.ds(pl.multiple_of(j * width, width), width)], held.at[j]
        if out:
            far, near = near, far
        return pltpu.make_async_copy(far, near, local_sem.at[which, j])

    def take_row(held, r):
        return jnp.stack([held[j, pl.ds(r, chains, stride=rows), :] for j in range(per)])

    def put_row(held, r, value):
        for j in range(per):
            held[j, pl.ds(r, chains, stride=rows), :] = value[j]

    def start_panels(whole, held, which, out=False):
        @pl.loop(0, per)
        def _(j):
            panel(whole, held, which, j, out).start()

    def wait_panels(whole, held, which, out=False):
        @pl.loop(0, per)
        def _(j):
            panel(whole, held, which, j, out).wait()

    @pl.loop(0, per)
    def _(j):
        panel(xin_ref, xheld, 0, j).wait()
        for r in range(rows):
            x_ref[r * per + j] = xheld[j, pl.ds(r, chains, stride=rows), :]

    small = [
        pltpu.make_async_copy(far, near, small_sem.at[i])
        for i, (far, near) in enumerate(
            (
                (kb_in, kb_ref),
                (vert_in, vert_ref),
                (match_in, match_ref),
                (counts_in, counts_ref),
                (exposure_in, exposure_ref),
                (diag_in, diag_ref),
            )
        )
    ]
    for copy in small:
        copy.start()
    start_panels(pin_ref, pheld, 1)
    pl.semaphore_wait(barrier, n - 1)

    def edge_copy(src, phase, down):
        where = blocks - per if down else 0
        side = 0 if down else 1
        peer = lax.rem(me + (1 if down else n - 1), n)
        return pltpu.make_async_remote_copy(
            src_ref=src.at[pl.ds(where, per)],
            dst_ref=halos[phase].at[side],
            send_sem=edge_send.at[phase, side],
            recv_sem=edge_recv.at[phase, side],
            device_id={"row": peer},
            device_id_type=MESH,
        )

    def start_edges(src, phase):
        @pl.when(me < n - 1)
        def _():
            edge_copy(src, phase, True).start()

        @pl.when(me > 0)
        def _():
            edge_copy(src, phase, False).start()

    def wait_edges(src, phase):
        @pl.when(me > 0)
        def _():
            edge_copy(src, phase, True).wait_recv()

        @pl.when(me < n - 1)
        def _():
            edge_copy(src, phase, False).wait_recv()

    def drain_edges(src, phase):
        @pl.when(me < n - 1)
        def _():
            edge_copy(src, phase, True).wait_send()

        @pl.when(me > 0)
        def _():
            edge_copy(src, phase, False).wait_send()

    def slab_copy(phase, peer, here, there):
        return pltpu.make_async_remote_copy(
            src_ref=sends[phase].at[pl.ds(peer * pairs, pairs)],
            dst_ref=recvs[phase].at[pl.ds(here * pairs, pairs)],
            send_sem=send_sem.at[phase, peer],
            recv_sem=recv_sem.at[phase, there],
            device_id={"row": peer},
            device_id_type=MESH,
        )

    early = n // 2

    def start_exchange(src, phase, first, last):
        @pl.loop(first, last)
        def _(k):
            peer = lax.rem(me + 1 + k, n)
            for i in range(pairs):
                sends[phase][peer * pairs + i] = src[order_ref[peer * pairs + i]]
            slab_copy(phase, peer, me, me).start()

        if first == 0:
            for i in range(pairs):
                recvs[phase][me * pairs + i] = src[order_ref[me * pairs + i]]

    def wait_exchange(phase):
        @pl.loop(1, n)
        def _(d):
            peer = lax.rem(me + d, n)
            slab_copy(phase, peer, me, peer).wait_recv()

    def drain_exchange(phase):
        @pl.loop(1, n)
        def _(d):
            peer = lax.rem(me + d, n)
            slab_copy(phase, peer, me, me).wait_send()

    start_edges(x_ref, 0)
    start_exchange(x_ref, 0, 0, n - 1)

    for copy in small:
        copy.wait()
    for q in range(kinds):
        high, low = split(kb_ref[q])
        kh_ref[:width, q * width : (q + 1) * width] = high
        kh_ref[width:, q * width : (q + 1) * width] = high
        kl_ref[:, q * width : (q + 1) * width] = low
    high, low = split(vert_ref[...].T)
    uh_ref[:width] = high
    ul_ref[:width] = low
    high, low = split(vert_ref[...])
    uh_ref[width:] = high
    ul_ref[width:] = low
    high, low = split(match_ref[...])
    mh_ref[:width] = high
    mh_ref[width:] = high
    ml_ref[...] = low

    tile = (per, chains, width)
    chain = lax.broadcasted_iota(jnp.int32, (chains, width), 0)
    step = jnp.zeros((chains, width), f32)
    for c in range(chains):
        step = jnp.where(chain == c, step_ref[c], step)
    step = step[None]

    def unit_row(src, r):
        line = src[pl.ds(r, 1), :]
        return jnp.stack(
            [
                jnp.broadcast_to(line[:, j * width : (j + 1) * width], (chains, width))
                for j in range(per)
            ]
        )

    def times_match(value):
        high, low = split(value)
        both = jnp.concatenate([high, low], axis=1)
        return dot(both, mh_ref[...]) + dot(high, ml_ref[...])

    def fill(src):
        @pl.loop(0, rows)
        def _(r):
            high, low = split(src[pl.ds(r * per, per)].reshape(lines, width))
            vh_ref[pl.ds((r + 1) * lines, lines)] = high
            vl_ref[pl.ds((r + 1) * lines, lines)] = low

    def fill_halo(phase):
        for side, outside in ((0, me == 0), (1, me == n - 1)):
            value = halos[phase][side].reshape(lines, width)
            value = jnp.where(outside, jnp.zeros_like(value), value)
            high, low = split(value)
            at = side * (rows + 1) * lines
            vh_ref[at : at + lines] = high
            vl_ref[at : at + lines] = low

    def local_grad(src, r):
        here = pl.ds(r * per, per)
        vh = vh_ref[pl.ds((r + 1) * lines, lines)]
        vl = vl_ref[pl.ds((r + 1) * lines, lines)]
        within = dot(jnp.concatenate([vh, vl], axis=1), kh_ref[...]) + dot(vh, kl_ref[...])
        kind = jnp.stack([jnp.full((chains, width), kind_ref[r, j]) for j in range(per)])
        own = within[:, :width].reshape(tile)
        for q in range(1, kinds):
            own = jnp.where(kind == q, within[:, q * width : (q + 1) * width].reshape(tile), own)
        above, below = pl.ds(r * lines, lines), pl.ds((r + 2) * lines, lines)
        sh = jnp.concatenate([vh_ref[below], vh_ref[above]], axis=1)
        sl = jnp.concatenate([vl_ref[below], vl_ref[above]], axis=1)
        vertical = dot(sh, uh_ref[...]) + dot(sl, uh_ref[...]) + dot(sh, ul_ref[...])
        value = src[here]
        return (
            own
            - vertical.reshape(tile)
            + unit_row(diag_ref, r) * value
            - unit_row(counts_ref, r)
            + unit_row(exposure_ref, r) * jnp.exp(value)
        )

    def all_rows(src, phase, use):
        fill(src)

        @pl.loop(1, rows - 1)
        def _(r):
            use(r, local_grad(src, r))

        wait_edges(src, phase)
        fill_halo(phase)

        @pl.loop(0, 2)
        def _(e):
            r = e * (rows - 1)
            use(r, local_grad(src, r))

    def received(phase, r):
        return jnp.concatenate(
            [recvs[phase][pos_ref[r * per + i]] for i in range(per)], axis=0
        )

    def use_first(r, grad):
        here = pl.ds(r * per, per)
        half = take_row(pheld, r) - 0.5 * step * grad
        half_ref[here] = half
        w_ref[here] = x_ref[here] + step * half

    wait_panels(pin_ref, pheld, 1)
    all_rows(x_ref, 0, use_first)
    start_exchange(w_ref, 1, 0, early)

    @pl.loop(0, rows)
    def _(r):
        here = pl.ds(r * per, per)
        product = times_match(x_ref[here].reshape(lines, width)).reshape(tile)
        q1_ref[here] = 0.5 * step * step * product

    wait_exchange(0)

    @pl.loop(0, rows)
    def _(r):
        here = pl.ds(r * per, per)
        matched = times_match(received(0, r)).reshape(tile)
        half_ref[here] = half_ref[here] + 0.5 * step * matched
        moved_ref[here] = w_ref[here] + 0.5 * step * step * matched

    start_edges(moved_ref, 1)
    start_exchange(w_ref, 1, early, n - 1)

    def use_second(r, grad):
        here = pl.ds(r * per, per)
        full = half_ref[here] - step * grad
        wfull_ref[here] = full
        w2_ref[here] = moved_ref[here] + step * full

    all_rows(moved_ref, 1, use_second)
    start_exchange(w2_ref, 2, 0, early)

    @pl.loop(0, rows)
    def _(r):
        here = pl.ds(r * per, per)
        product = times_match(moved_ref[here].reshape(lines, width)).reshape(tile)
        q2_ref[here] = step * step * product

    wait_exchange(1)

    @pl.loop(0, rows)
    def _(r):
        here = pl.ds(r * per, per)
        value = received(1, r) + q1_ref[here].reshape(lines, width)
        matched = times_match(value).reshape(tile)
        wfull_ref[here] = wfull_ref[here] + step * matched
        newx = w2_ref[here] + step * step * matched
        newx_ref[here] = newx
        put_row(xoheld, r, newx)

    start_edges(newx_ref, 2)
    start_exchange(w2_ref, 2, early, n - 1)
    start_panels(xout_ref, xoheld, 2, True)

    def use_third(r, grad):
        here = pl.ds(r * per, per)
        newp_ref[here] = wfull_ref[here] - 0.5 * step * grad

    all_rows(newx_ref, 2, use_third)
    wait_exchange(2)

    @pl.loop(0, rows)
    def _(r):
        here = pl.ds(r * per, per)
        value = received(2, r) + q2_ref[here].reshape(lines, width)
        matched = times_match(value).reshape(tile)
        put_row(poheld, r, newp_ref[here] + 0.5 * step * matched)

    start_panels(pout_ref, poheld, 3, True)
    for phase, src in enumerate((x_ref, moved_ref, newx_ref)):
        drain_edges(src, phase)
        drain_exchange(phase)
    wait_panels(xout_ref, xoheld, 2, True)
    wait_panels(pout_ref, poheld, 3, True)


def body(
    positions,
    momenta,
    step_size,
    counts,
    exposure,
    precision_diag,
    kind_blocks,
    vertical_coupling,
    matched_coupling,
    partner,
    block_kind,
):
    n = lax.axis_size("row")
    chains, rows, cols = positions.shape
    kinds, width = kind_blocks.shape[:2]
    per = cols // width
    blocks = rows * per

    ids = jnp.arange(blocks, dtype=jnp.int32)
    key = (partner // blocks) * blocks + ids
    slot = jnp.sum((key[None, :] < key[:, None]).astype(jnp.int32), axis=1)
    pos = jnp.sum((partner[None, :] < partner[:, None]).astype(jnp.int32), axis=1)
    order = jnp.sum(jnp.where(slot[None, :] == ids[:, None], ids[None, :], 0), axis=1)

    hbm = pl.BlockSpec(memory_space=pl.ANY)
    smem = pl.BlockSpec(memory_space=pltpu.SMEM)
    field = (blocks, chains, width)
    lines = per * chains
    big = lambda: pltpu.VMEM(field, f32)
    flat = (chains * rows, cols)
    newx, newp = pl.pallas_call(
        functools.partial(kernel, n),
        out_shape=(jax.ShapeDtypeStruct(flat, f32), jax.ShapeDtypeStruct(flat, f32)),
        in_specs=[smem] * 4 + [hbm] * 8,
        out_specs=(hbm, hbm),
        scratch_shapes=[big() for _ in range(10)]
        + [
            pltpu.VMEM(((rows + 2) * lines, width), bf16),
            pltpu.VMEM(((rows + 2) * lines, width), bf16),
            pltpu.VMEM((2 * width, kinds * width), bf16),
            pltpu.VMEM((width, kinds * width), bf16),
            pltpu.VMEM((2 * width, width), bf16),
            pltpu.VMEM((2 * width, width), bf16),
            pltpu.VMEM((2 * width, width), bf16),
            pltpu.VMEM((width, width), bf16),
        ]
        + [big() for _ in range(6)]
        + [pltpu.VMEM((2, per, chains, width), f32) for _ in range(3)]
        + [
            pltpu.SemaphoreType.DMA((3, n)),
            pltpu.SemaphoreType.DMA((3, n)),
            pltpu.SemaphoreType.DMA((3, 2)),
            pltpu.SemaphoreType.DMA((3, 2)),
        ]
        + [pltpu.VMEM((per, chains * rows, width), f32) for _ in range(4)]
        + [pltpu.SemaphoreType.DMA((4, per))]
        + [pltpu.VMEM((rows, cols), f32) for _ in range(3)]
        + [
            pltpu.VMEM((kinds, width, width), f32),
            pltpu.VMEM((width, width), f32),
            pltpu.VMEM((width, width), f32),
            pltpu.SemaphoreType.DMA((6,)),
        ],
        compiler_params=pltpu.CompilerParams(
            collective_id=0, has_side_effects=True, vmem_limit_bytes=60 * 1024 * 1024
        ),
    )(
        order,
        pos,
        step_size,
        block_kind,
        positions.reshape(flat),
        momenta.reshape(flat),
        counts,
        exposure,
        precision_diag,
        kind_blocks,
        vertical_coupling,
        matched_coupling,
    )
    return newx.reshape(positions.shape), newp.reshape(positions.shape)


def solution(mesh):
    return jax.shard_map(
        body,
        mesh=mesh,
        in_specs=(
            P(None, ("groups", "row"), None),
            P(None, ("groups", "row"), None),
            P("groups"),
            P(("groups", "row"), None),
            P(("groups", "row"), None),
            P(("groups", "row"), None),
            P(),
            P(),
            P(),
            P(("groups", "row")),
            P(("groups", "row"), None),
        ),
        out_specs=(P(None, ("groups", "row"), None), P(None, ("groups", "row"), None)),
        check_vma=False,
    )
```

```python
import functools

import jax
import jax.numpy as jnp
from jax import lax
from jax.experimental import pallas as pl
from jax.experimental.pallas import tpu as pltpu
from jax.sharding import PartitionSpec as P

MESH = pl.DeviceIdType.MESH
bf16 = jnp.bfloat16
f32 = jnp.float32


def split(value):
    high = value.astype(bf16)
    low = (value - high.astype(f32)).astype(bf16)
    return high, low


def dot(a, b):
    return jnp.dot(a, b, preferred_element_type=f32)


def kernel(
    n,
    order_ref,
    pos_ref,
    step_ref,
    kind_ref,
    xin_ref,
    pin_ref,
    counts_in,
    exposure_in,
    diag_in,
    kb_in,
    vert_in,
    match_in,
    xout_ref,
    pout_ref,
    x_ref,
    newx_ref,
    newp_ref,
    half_ref,
    w_ref,
    moved_ref,
    wfull_ref,
    w2_ref,
    q1_ref,
    q2_ref,
    vh_ref,
    vl_ref,
    kh_ref,
    kl_ref,
    uh_ref,
    ul_ref,
    mh_ref,
    ml_ref,
    send0,
    send1,
    send2,
    recv0,
    recv1,
    recv2,
    halo0,
    halo1,
    halo2,
    send_sem,
    recv_sem,
    edge_send,
    edge_recv,
    xheld,
    pheld,
    xoheld,
    poheld,
    local_sem,
    counts_ref,
    exposure_ref,
    diag_ref,
    kb_ref,
    vert_ref,
    match_ref,
    small_sem,
):
    me = lax.axis_index("row")
    blocks, chains, width = x_ref.shape
    kinds = kb_ref.shape[0]
    rows, per = kind_ref.shape
    lines = per * chains
    pairs = blocks // n
    sends = (send0, send1, send2)
    recvs = (recv0, recv1, recv2)
    halos = (halo0, halo1, halo2)

    barrier = pltpu.get_barrier_semaphore()

    @pl.loop(0, per)
    def _(j):
        pltpu.make_async_copy(
            xin_ref.at[:, pl.ds(pl.multiple_of(j * width, width), width)],
            xheld.at[j],
            local_sem.at[0, j],
        ).start()

    @pl.loop(1, n)
    def _(d):
        pl.semaphore_signal(
            barrier, inc=1, device_id={"row": lax.rem(me + d, n)}, device_id_type=MESH
        )

    def panel(whole, held, which, j, out=False):
        far, near = whole.at[:, pl.ds(pl.multiple_of(j * width, width), width)], held.at[j]
        if out:
            far, near = near, far
        return pltpu.make_async_copy(far, near, local_sem.at[which, j])

    def take_row(held, r):
        return jnp.stack([held[j, pl.ds(r, chains, stride=rows), :] for j in range(per)])

    def put_row(held, r, value):
        for j in range(per):
            held[j, pl.ds(r, chains, stride=rows), :] = value[j]

    def start_panels(whole, held, which, out=False):
        @pl.loop(0, per)
        def _(j):
            panel(whole, held, which, j, out).start()

    def wait_panels(whole, held, which, out=False):
        @pl.loop(0, per)
        def _(j):
            panel(whole, held, which, j, out).wait()

    @pl.loop(0, per)
    def _(j):
        panel(xin_ref, xheld, 0, j).wait()
        for r in range(rows):
            x_ref[r * per + j] = xheld[j, pl.ds(r, chains, stride=rows), :]

    small = [
        pltpu.make_async_copy(far, near, small_sem.at[i])
        for i, (far, near) in enumerate(
            (
                (kb_in, kb_ref),
                (vert_in, vert_ref),
                (match_in, match_ref),
                (counts_in, counts_ref),
                (exposure_in, exposure_ref),
                (diag_in, diag_ref),
            )
        )
    ]
    for copy in small:
        copy.start()
    start_panels(pin_ref, pheld, 1)
    pl.semaphore_wait(barrier, n - 1)

    def edge_copy(src, phase, down):
        where = blocks - per if down else 0
        side = 0 if down else 1
        peer = lax.rem(me + (1 if down else n - 1), n)
        return pltpu.make_async_remote_copy(
            src_ref=src.at[pl.ds(where, per)],
            dst_ref=halos[phase].at[side],
            send_sem=edge_send.at[phase, side],
            recv_sem=edge_recv.at[phase, side],
            device_id={"row": peer},
            device_id_type=MESH,
        )

    def start_edges(src, phase):
        @pl.when(me < n - 1)
        def _():
            edge_copy(src, phase, True).start()

        @pl.when(me > 0)
        def _():
            edge_copy(src, phase, False).start()

    def wait_edges(src, phase):
        @pl.when(me > 0)
        def _():
            edge_copy(src, phase, True).wait_recv()

        @pl.when(me < n - 1)
        def _():
            edge_copy(src, phase, False).wait_recv()

    def drain_edges(src, phase):
        @pl.when(me < n - 1)
        def _():
            edge_copy(src, phase, True).wait_send()

        @pl.when(me > 0)
        def _():
            edge_copy(src, phase, False).wait_send()

    def slab_copy(phase, peer, here, there):
        return pltpu.make_async_remote_copy(
            src_ref=sends[phase].at[pl.ds(peer * pairs, pairs)],
            dst_ref=recvs[phase].at[pl.ds(here * pairs, pairs)],
            send_sem=send_sem.at[phase, peer],
            recv_sem=recv_sem.at[phase, there],
            device_id={"row": peer},
            device_id_type=MESH,
        )

    early = n // 2

    def start_exchange(src, phase, first, last):
        @pl.loop(first, last)
        def _(k):
            peer = lax.rem(me + 1 + k, n)
            for i in range(pairs):
                sends[phase][peer * pairs + i] = src[order_ref[peer * pairs + i]]
            slab_copy(phase, peer, me, me).start()

        if first == 0:
            for i in range(pairs):
                recvs[phase][me * pairs + i] = src[order_ref[me * pairs + i]]

    def wait_exchange(phase):
        @pl.loop(1, n)
        def _(d):
            peer = lax.rem(me + d, n)
            slab_copy(phase, peer, me, peer).wait_recv()

    def drain_exchange(phase):
        @pl.loop(1, n)
        def _(d):
            peer = lax.rem(me + d, n)
            slab_copy(phase, peer, me, me).wait_send()

    start_edges(x_ref, 0)
    start_exchange(x_ref, 0, 0, n - 1)

    for copy in small:
        copy.wait()
    for q in range(kinds):
        high, low = split(kb_ref[q])
        kh_ref[:width, q * width : (q + 1) * width] = high
        kh_ref[width:, q * width : (q + 1) * width] = high
        kl_ref[:, q * width : (q + 1) * width] = low
    high, low = split(vert_ref[...].T)
    uh_ref[:width] = high
    ul_ref[:width] = low
    high, low = split(vert_ref[...])
    uh_ref[width:] = high
    ul_ref[width:] = low
    high, low = split(match_ref[...])
    mh_ref[:width] = high
    mh_ref[width:] = high
    ml_ref[...] = low

    tile = (per, chains, width)
    chain = lax.broadcasted_iota(jnp.int32, (chains, width), 0)
    step = jnp.zeros((chains, width), f32)
    for c in range(chains):
        step = jnp.where(chain == c, step_ref[c], step)
    step = step[None]

    def unit_row(src, r):
        line = src[pl.ds(r, 1), :]
        return jnp.stack(
            [
                jnp.broadcast_to(line[:, j * width : (j + 1) * width], (chains, width))
                for j in range(per)
            ]
        )

    def times_match(value):
        high, low = split(value)
        both = jnp.concatenate([high, low], axis=1)
        return dot(both, mh_ref[...]) + dot(high, ml_ref[...])

    def fill(src):
        @pl.loop(0, rows)
        def _(r):
            high, low = split(src[pl.ds(r * per, per)].reshape(lines, width))
            vh_ref[pl.ds((r + 1) * lines, lines)] = high
            vl_ref[pl.ds((r + 1) * lines, lines)] = low

    def fill_halo(phase):
        for side, outside in ((0, me == 0), (1, me == n - 1)):
            value = halos[phase][side].reshape(lines, width)
            value = jnp.where(outside, jnp.zeros_like(value), value)
            high, low = split(value)
            at = side * (rows + 1) * lines
            vh_ref[at : at + lines] = high
            vl_ref[at : at + lines] = low

    def local_grad(src, r):
        here = pl.ds(r * per, per)
        vh = vh_ref[pl.ds((r + 1) * lines, lines)]
        vl = vl_ref[pl.ds((r + 1) * lines, lines)]
        within = dot(jnp.concatenate([vh, vl], axis=1), kh_ref[...]) + dot(vh, kl_ref[...])
        kind = jnp.stack([jnp.full((chains, width), kind_ref[r, j]) for j in range(per)])
        own = within[:, :width].reshape(tile)
        for q in range(1, kinds):
            own = jnp.where(kind == q, within[:, q * width : (q + 1) * width].reshape(tile), own)
        above, below = pl.ds(r * lines, lines), pl.ds((r + 2) * lines, lines)
        sh = jnp.concatenate([vh_ref[below], vh_ref[above]], axis=1)
        sl = jnp.concatenate([vl_ref[below], vl_ref[above]], axis=1)
        vertical = dot(sh, uh_ref[...]) + dot(sl, uh_ref[...]) + dot(sh, ul_ref[...])
        value = src[here]
        return (
            own
            - vertical.reshape(tile)
            + unit_row(diag_ref, r) * value
            - unit_row(counts_ref, r)
            + unit_row(exposure_ref, r) * jnp.exp(value)
        )

    def all_rows(src, phase, use):
        fill(src)

        @pl.loop(1, rows - 1)
        def _(r):
            use(r, local_grad(src, r))

        wait_edges(src, phase)
        fill_halo(phase)

        @pl.loop(0, 2)
        def _(e):
            r = e * (rows - 1)
            use(r, local_grad(src, r))

    def received(phase, r):
        return jnp.concatenate(
            [recvs[phase][pos_ref[r * per + i]] for i in range(per)], axis=0
        )

    def use_first(r, grad):
        here = pl.ds(r * per, per)
        half = take_row(pheld, r) - 0.5 * step * grad
        half_ref[here] = half
        w_ref[here] = x_ref[here] + step * half

    wait_panels(pin_ref, pheld, 1)
    all_rows(x_ref, 0, use_first)
    start_exchange(w_ref, 1, 0, early)

    @pl.loop(0, rows)
    def _(r):
        here = pl.ds(r * per, per)
        product = times_match(x_ref[here].reshape(lines, width)).reshape(tile)
        q1_ref[here] = 0.5 * step * step * product

    wait_exchange(0)

    @pl.loop(0, rows)
    def _(r):
        here = pl.ds(r * per, per)
        matched = times_match(received(0, r)).reshape(tile)
        half_ref[here] = half_ref[here] + 0.5 * step * matched
        moved_ref[here] = w_ref[here] + 0.5 * step * step * matched

    start_edges(moved_ref, 1)
    start_exchange(w_ref, 1, early, n - 1)

    def use_second(r, grad):
        here = pl.ds(r * per, per)
        full = half_ref[here] - step * grad
        wfull_ref[here] = full
        ahead = moved_ref[here] + step * full
        w2_ref[here] = ahead
        half_ref[here] = times_match(ahead.reshape(lines, width)).reshape(tile)

    all_rows(moved_ref, 1, use_second)
    start_exchange(half_ref, 2, 0, early)

    @pl.loop(0, rows)
    def _(r):
        here = pl.ds(r * per, per)
        product = times_match(moved_ref[here].reshape(lines, width)).reshape(tile)
        twice = times_match((step * step * product).reshape(lines, width)).reshape(tile)
        q2_ref[here] = 0.5 * step * twice

    wait_exchange(1)

    @pl.loop(0, rows)
    def _(r):
        here = pl.ds(r * per, per)
        value = received(1, r) + q1_ref[here].reshape(lines, width)
        matched = times_match(value).reshape(tile)
        wfull_ref[here] = wfull_ref[here] + step * matched
        newx = w2_ref[here] + step * step * matched
        newx_ref[here] = newx
        put_row(xoheld, r, newx)

    start_edges(newx_ref, 2)
    start_exchange(half_ref, 2, early, n - 1)
    start_panels(xout_ref, xoheld, 2, True)

    def use_third(r, grad):
        here = pl.ds(r * per, per)
        newp_ref[here] = wfull_ref[here] + q2_ref[here] - 0.5 * step * grad

    all_rows(newx_ref, 2, use_third)
    wait_exchange(2)

    @pl.loop(0, rows)
    def _(r):
        here = pl.ds(r * per, per)
        matched = received(2, r).reshape(tile)
        put_row(poheld, r, newp_ref[here] + 0.5 * step * matched)

    start_panels(pout_ref, poheld, 3, True)
    for phase, src in enumerate((x_ref, moved_ref, newx_ref)):
        drain_edges(src, phase)
        drain_exchange(phase)
    wait_panels(xout_ref, xoheld, 2, True)
    wait_panels(pout_ref, poheld, 3, True)


def body(
    positions,
    momenta,
    step_size,
    counts,
    exposure,
    precision_diag,
    kind_blocks,
    vertical_coupling,
    matched_coupling,
    partner,
    block_kind,
):
    n = lax.axis_size("row")
    chains, rows, cols = positions.shape
    kinds, width = kind_blocks.shape[:2]
    per = cols // width
    blocks = rows * per

    ids = jnp.arange(blocks, dtype=jnp.int32)
    key = (partner // blocks) * blocks + ids
    slot = jnp.sum((key[None, :] < key[:, None]).astype(jnp.int32), axis=1)
    pos = jnp.sum((partner[None, :] < partner[:, None]).astype(jnp.int32), axis=1)
    order = jnp.sum(jnp.where(slot[None, :] == ids[:, None], ids[None, :], 0), axis=1)

    hbm = pl.BlockSpec(memory_space=pl.ANY)
    smem = pl.BlockSpec(memory_space=pltpu.SMEM)
    field = (blocks, chains, width)
    lines = per * chains
    big = lambda: pltpu.VMEM(field, f32)
    flat = (chains * rows, cols)
    newx, newp = pl.pallas_call(
        functools.partial(kernel, n),
        out_shape=(jax.ShapeDtypeStruct(flat, f32), jax.ShapeDtypeStruct(flat, f32)),
        in_specs=[smem] * 4 + [hbm] * 8,
        out_specs=(hbm, hbm),
        scratch_shapes=[big() for _ in range(10)]
        + [
            pltpu.VMEM(((rows + 2) * lines, width), bf16),
            pltpu.VMEM(((rows + 2) * lines, width), bf16),
            pltpu.VMEM((2 * width, kinds * width), bf16),
            pltpu.VMEM((width, kinds * width), bf16),
            pltpu.VMEM((2 * width, width), bf16),
            pltpu.VMEM((2 * width, width), bf16),
            pltpu.VMEM((2 * width, width), bf16),
            pltpu.VMEM((width, width), bf16),
        ]
        + [big() for _ in range(6)]
        + [pltpu.VMEM((2, per, chains, width), f32) for _ in range(3)]
        + [
            pltpu.SemaphoreType.DMA((3, n)),
            pltpu.SemaphoreType.DMA((3, n)),
            pltpu.SemaphoreType.DMA((3, 2)),
            pltpu.SemaphoreType.DMA((3, 2)),
        ]
        + [pltpu.VMEM((per, chains * rows, width), f32) for _ in range(4)]
        + [pltpu.SemaphoreType.DMA((4, per))]
        + [pltpu.VMEM((rows, cols), f32) for _ in range(3)]
        + [
            pltpu.VMEM((kinds, width, width), f32),
            pltpu.VMEM((width, width), f32),
            pltpu.VMEM((width, width), f32),
            pltpu.SemaphoreType.DMA((6,)),
        ],
        compiler_params=pltpu.CompilerParams(
            collective_id=0, has_side_effects=True, vmem_limit_bytes=60 * 1024 * 1024
        ),
    )(
        order,
        pos,
        step_size,
        block_kind,
        positions.reshape(flat),
        momenta.reshape(flat),
        counts,
        exposure,
        precision_diag,
        kind_blocks,
        vertical_coupling,
        matched_coupling,
    )
    return newx.reshape(positions.shape), newp.reshape(positions.shape)


def solution(mesh):
    return jax.shard_map(
        body,
        mesh=mesh,
        in_specs=(
            P(None, ("groups", "row"), None),
            P(None, ("groups", "row"), None),
            P("groups"),
            P(("groups", "row"), None),
            P(("groups", "row"), None),
            P(("groups", "row"), None),
            P(),
            P(),
            P(),
            P(("groups", "row")),
            P(("groups", "row"), None),
        ),
        out_specs=(P(None, ("groups", "row"), None), P(None, ("groups", "row"), None)),
        check_vma=False,
    )
```

```python
import functools

import jax
import jax.numpy as jnp
from jax import lax
from jax.experimental import pallas as pl
from jax.experimental.pallas import tpu as pltpu
from jax.sharding import PartitionSpec as P

MESH = pl.DeviceIdType.MESH
bf16 = jnp.bfloat16
f32 = jnp.float32


def split(value):
    high = value.astype(bf16)
    low = (value - high.astype(f32)).astype(bf16)
    return high, low


def dot(a, b):
    return jnp.dot(a, b, preferred_element_type=f32)


def kernel(
    n,
    order_ref,
    pos_ref,
    step_ref,
    kind_ref,
    xin_ref,
    pin_ref,
    counts_in,
    exposure_in,
    diag_in,
    kb_in,
    vert_in,
    match_in,
    xout_ref,
    pout_ref,
    x_ref,
    newx_ref,
    newp_ref,
    half_ref,
    wm_ref,
    w_ref,
    moved_ref,
    wfull_ref,
    w2_ref,
    q1_ref,
    q2_ref,
    vh_ref,
    vl_ref,
    kh_ref,
    kl_ref,
    uh_ref,
    ul_ref,
    mh_ref,
    ml_ref,
    send0,
    send1,
    send2,
    recv0,
    recv1,
    recv2,
    halo0,
    halo1,
    halo2,
    send_sem,
    recv_sem,
    edge_send,
    edge_recv,
    xheld,
    pheld,
    xoheld,
    poheld,
    local_sem,
    counts_ref,
    exposure_ref,
    diag_ref,
    kb_ref,
    vert_ref,
    match_ref,
    small_sem,
):
    me = lax.axis_index("row")
    blocks, chains, width = x_ref.shape
    kinds = kb_ref.shape[0]
    rows, per = kind_ref.shape
    lines = per * chains
    pairs = blocks // n
    sends = (send0, send1, send2)
    recvs = (recv0, recv1, recv2)
    halos = (halo0, halo1, halo2)

    barrier = pltpu.get_barrier_semaphore()

    @pl.loop(0, per)
    def _(j):
        pltpu.make_async_copy(
            xin_ref.at[:, pl.ds(pl.multiple_of(j * width, width), width)],
            xheld.at[j],
            local_sem.at[0, j],
        ).start()

    @pl.loop(1, n)
    def _(d):
        pl.semaphore_signal(
            barrier, inc=1, device_id={"row": lax.rem(me + d, n)}, device_id_type=MESH
        )

    def panel(whole, held, which, j, out=False):
        far, near = whole.at[:, pl.ds(pl.multiple_of(j * width, width), width)], held.at[j]
        if out:
            far, near = near, far
        return pltpu.make_async_copy(far, near, local_sem.at[which, j])

    def take_row(held, r):
        return jnp.stack([held[j, pl.ds(r, chains, stride=rows), :] for j in range(per)])

    def put_row(held, r, value):
        for j in range(per):
            held[j, pl.ds(r, chains, stride=rows), :] = value[j]

    def start_panels(whole, held, which, out=False):
        @pl.loop(0, per)
        def _(j):
            panel(whole, held, which, j, out).start()

    def wait_panels(whole, held, which, out=False):
        @pl.loop(0, per)
        def _(j):
            panel(whole, held, which, j, out).wait()

    @pl.loop(0, per)
    def _(j):
        panel(xin_ref, xheld, 0, j).wait()
        for r in range(rows):
            x_ref[r * per + j] = xheld[j, pl.ds(r, chains, stride=rows), :]

    small = [
        pltpu.make_async_copy(far, near, small_sem.at[i])
        for i, (far, near) in enumerate(
            (
                (kb_in, kb_ref),
                (vert_in, vert_ref),
                (match_in, match_ref),
                (counts_in, counts_ref),
                (exposure_in, exposure_ref),
                (diag_in, diag_ref),
            )
        )
    ]
    for copy in small:
        copy.start()
    start_panels(pin_ref, pheld, 1)
    pl.semaphore_wait(barrier, n - 1)

    def edge_copy(src, phase, down):
        where = blocks - per if down else 0
        side = 0 if down else 1
        peer = lax.rem(me + (1 if down else n - 1), n)
        return pltpu.make_async_remote_copy(
            src_ref=src.at[pl.ds(where, per)],
            dst_ref=halos[phase].at[side],
            send_sem=edge_send.at[phase, side],
            recv_sem=edge_recv.at[phase, side],
            device_id={"row": peer},
            device_id_type=MESH,
        )

    def start_edges(src, phase):
        @pl.when(me < n - 1)
        def _():
            edge_copy(src, phase, True).start()

        @pl.when(me > 0)
        def _():
            edge_copy(src, phase, False).start()

    def wait_edges(src, phase):
        @pl.when(me > 0)
        def _():
            edge_copy(src, phase, True).wait_recv()

        @pl.when(me < n - 1)
        def _():
            edge_copy(src, phase, False).wait_recv()

    def drain_edges(src, phase):
        @pl.when(me < n - 1)
        def _():
            edge_copy(src, phase, True).wait_send()

        @pl.when(me > 0)
        def _():
            edge_copy(src, phase, False).wait_send()

    def slab_copy(phase, peer, here, there):
        return pltpu.make_async_remote_copy(
            src_ref=sends[phase].at[pl.ds(peer * pairs, pairs)],
            dst_ref=recvs[phase].at[pl.ds(here * pairs, pairs)],
            send_sem=send_sem.at[phase, peer],
            recv_sem=recv_sem.at[phase, there],
            device_id={"row": peer},
            device_id_type=MESH,
        )

    early = n // 2

    def start_exchange(src, phase, first, last):
        @pl.loop(first, last)
        def _(k):
            peer = lax.rem(me + 1 + k, n)
            for i in range(pairs):
                sends[phase][peer * pairs + i] = src[order_ref[peer * pairs + i]]
            slab_copy(phase, peer, me, me).start()

        if first == 0:
            for i in range(pairs):
                recvs[phase][me * pairs + i] = src[order_ref[me * pairs + i]]

    def wait_exchange(phase):
        @pl.loop(1, n)
        def _(d):
            peer = lax.rem(me + d, n)
            slab_copy(phase, peer, me, peer).wait_recv()

    def drain_exchange(phase):
        @pl.loop(1, n)
        def _(d):
            peer = lax.rem(me + d, n)
            slab_copy(phase, peer, me, me).wait_send()

    start_edges(x_ref, 0)
    start_exchange(x_ref, 0, 0, n - 1)

    for copy in small:
        copy.wait()
    for q in range(kinds):
        high, low = split(kb_ref[q])
        kh_ref[:width, q * width : (q + 1) * width] = high
        kh_ref[width:, q * width : (q + 1) * width] = high
        kl_ref[:, q * width : (q + 1) * width] = low
    high, low = split(vert_ref[...].T)
    uh_ref[:width] = high
    ul_ref[:width] = low
    high, low = split(vert_ref[...])
    uh_ref[width:] = high
    ul_ref[width:] = low
    high, low = split(match_ref[...])
    mh_ref[:width] = high
    mh_ref[width:] = high
    ml_ref[...] = low

    tile = (per, chains, width)
    chain = lax.broadcasted_iota(jnp.int32, (chains, width), 0)
    step = jnp.zeros((chains, width), f32)
    for c in range(chains):
        step = jnp.where(chain == c, step_ref[c], step)
    step = step[None]

    def unit_row(src, r):
        line = src[pl.ds(r, 1), :]
        return jnp.stack(
            [
                jnp.broadcast_to(line[:, j * width : (j + 1) * width], (chains, width))
                for j in range(per)
            ]
        )

    def times_match(value):
        high, low = split(value)
        both = jnp.concatenate([high, low], axis=1)
        return dot(both, mh_ref[...]) + dot(high, ml_ref[...])

    def fill(src):
        @pl.loop(0, rows)
        def _(r):
            high, low = split(src[pl.ds(r * per, per)].reshape(lines, width))
            vh_ref[pl.ds((r + 1) * lines, lines)] = high
            vl_ref[pl.ds((r + 1) * lines, lines)] = low

    def fill_halo(phase):
        for side, outside in ((0, me == 0), (1, me == n - 1)):
            value = halos[phase][side].reshape(lines, width)
            value = jnp.where(outside, jnp.zeros_like(value), value)
            high, low = split(value)
            at = side * (rows + 1) * lines
            vh_ref[at : at + lines] = high
            vl_ref[at : at + lines] = low

    def local_grad(src, r):
        here = pl.ds(r * per, per)
        vh = vh_ref[pl.ds((r + 1) * lines, lines)]
        vl = vl_ref[pl.ds((r + 1) * lines, lines)]
        within = dot(jnp.concatenate([vh, vl], axis=1), kh_ref[...]) + dot(vh, kl_ref[...])
        kind = jnp.stack([jnp.full((chains, width), kind_ref[r, j]) for j in range(per)])
        own = within[:, :width].reshape(tile)
        for q in range(1, kinds):
            own = jnp.where(kind == q, within[:, q * width : (q + 1) * width].reshape(tile), own)
        above, below = pl.ds(r * lines, lines), pl.ds((r + 2) * lines, lines)
        sh = jnp.concatenate([vh_ref[below], vh_ref[above]], axis=1)
        sl = jnp.concatenate([vl_ref[below], vl_ref[above]], axis=1)
        vertical = dot(sh, uh_ref[...]) + dot(sl, uh_ref[...]) + dot(sh, ul_ref[...])
        value = src[here]
        return (
            own
            - vertical.reshape(tile)
            + unit_row(diag_ref, r) * value
            - unit_row(counts_ref, r)
            + unit_row(exposure_ref, r) * jnp.exp(value)
        )

    def all_rows(src, phase, use):
        fill(src)

        @pl.loop(1, rows - 1)
        def _(r):
            use(r, local_grad(src, r))

        wait_edges(src, phase)
        fill_halo(phase)

        @pl.loop(0, 2)
        def _(e):
            r = e * (rows - 1)
            use(r, local_grad(src, r))

    def received(phase, r):
        return jnp.concatenate(
            [recvs[phase][pos_ref[r * per + i]] for i in range(per)], axis=0
        )

    def use_first(r, grad):
        here = pl.ds(r * per, per)
        half = take_row(pheld, r) - 0.5 * step * grad
        half_ref[here] = half
        ahead = x_ref[here] + step * half
        w_ref[here] = ahead
        wm_ref[here] = times_match(ahead.reshape(lines, width)).reshape(tile)

    wait_panels(pin_ref, pheld, 1)
    all_rows(x_ref, 0, use_first)
    start_exchange(wm_ref, 1, 0, early)

    @pl.loop(0, rows)
    def _(r):
        here = pl.ds(r * per, per)
        product = times_match(x_ref[here].reshape(lines, width)).reshape(tile)
        twice = (0.5 * step * step * product).reshape(lines, width)
        q1_ref[here] = times_match(twice).reshape(tile)

    wait_exchange(0)

    @pl.loop(0, rows)
    def _(r):
        here = pl.ds(r * per, per)
        matched = times_match(received(0, r)).reshape(tile)
        half_ref[here] = half_ref[here] + 0.5 * step * matched
        moved_ref[here] = w_ref[here] + 0.5 * step * step * matched

    start_edges(moved_ref, 1)
    start_exchange(wm_ref, 1, early, n - 1)

    def use_second(r, grad):
        here = pl.ds(r * per, per)
        full = half_ref[here] - step * grad
        wfull_ref[here] = full
        ahead = moved_ref[here] + step * full
        w2_ref[here] = ahead
        half_ref[here] = times_match(ahead.reshape(lines, width)).reshape(tile)

    all_rows(moved_ref, 1, use_second)
    start_exchange(half_ref, 2, 0, early)

    @pl.loop(0, rows)
    def _(r):
        here = pl.ds(r * per, per)
        product = times_match(moved_ref[here].reshape(lines, width)).reshape(tile)
        twice = times_match((step * step * product).reshape(lines, width)).reshape(tile)
        q2_ref[here] = 0.5 * step * twice

    wait_exchange(1)

    @pl.loop(0, rows)
    def _(r):
        here = pl.ds(r * per, per)
        matched = received(1, r).reshape(tile) + q1_ref[here]
        wfull_ref[here] = wfull_ref[here] + step * matched
        newx = w2_ref[here] + step * step * matched
        newx_ref[here] = newx
        put_row(xoheld, r, newx)

    start_edges(newx_ref, 2)
    start_exchange(half_ref, 2, early, n - 1)
    start_panels(xout_ref, xoheld, 2, True)

    def use_third(r, grad):
        here = pl.ds(r * per, per)
        newp_ref[here] = wfull_ref[here] + q2_ref[here] - 0.5 * step * grad

    all_rows(newx_ref, 2, use_third)
    wait_exchange(2)

    @pl.loop(0, rows)
    def _(r):
        here = pl.ds(r * per, per)
        matched = received(2, r).reshape(tile)
        put_row(poheld, r, newp_ref[here] + 0.5 * step * matched)

    start_panels(pout_ref, poheld, 3, True)
    for phase, src in enumerate((x_ref, moved_ref, newx_ref)):
        drain_edges(src, phase)
        drain_exchange(phase)
    wait_panels(xout_ref, xoheld, 2, True)
    wait_panels(pout_ref, poheld, 3, True)


def body(
    positions,
    momenta,
    step_size,
    counts,
    exposure,
    precision_diag,
    kind_blocks,
    vertical_coupling,
    matched_coupling,
    partner,
    block_kind,
):
    n = lax.axis_size("row")
    chains, rows, cols = positions.shape
    kinds, width = kind_blocks.shape[:2]
    per = cols // width
    blocks = rows * per

    ids = jnp.arange(blocks, dtype=jnp.int32)
    key = (partner // blocks) * blocks + ids
    slot = jnp.sum((key[None, :] < key[:, None]).astype(jnp.int32), axis=1)
    pos = jnp.sum((partner[None, :] < partner[:, None]).astype(jnp.int32), axis=1)
    order = jnp.sum(jnp.where(slot[None, :] == ids[:, None], ids[None, :], 0), axis=1)

    hbm = pl.BlockSpec(memory_space=pl.ANY)
    smem = pl.BlockSpec(memory_space=pltpu.SMEM)
    field = (blocks, chains, width)
    lines = per * chains
    big = lambda: pltpu.VMEM(field, f32)
    flat = (chains * rows, cols)
    newx, newp = pl.pallas_call(
        functools.partial(kernel, n),
        out_shape=(jax.ShapeDtypeStruct(flat, f32), jax.ShapeDtypeStruct(flat, f32)),
        in_specs=[smem] * 4 + [hbm] * 8,
        out_specs=(hbm, hbm),
        scratch_shapes=[big() for _ in range(11)]
        + [
            pltpu.VMEM(((rows + 2) * lines, width), bf16),
            pltpu.VMEM(((rows + 2) * lines, width), bf16),
            pltpu.VMEM((2 * width, kinds * width), bf16),
            pltpu.VMEM((width, kinds * width), bf16),
            pltpu.VMEM((2 * width, width), bf16),
            pltpu.VMEM((2 * width, width), bf16),
            pltpu.VMEM((2 * width, width), bf16),
            pltpu.VMEM((width, width), bf16),
        ]
        + [big() for _ in range(6)]
        + [pltpu.VMEM((2, per, chains, width), f32) for _ in range(3)]
        + [
            pltpu.SemaphoreType.DMA((3, n)),
            pltpu.SemaphoreType.DMA((3, n)),
            pltpu.SemaphoreType.DMA((3, 2)),
            pltpu.SemaphoreType.DMA((3, 2)),
        ]
        + [pltpu.VMEM((per, chains * rows, width), f32) for _ in range(4)]
        + [pltpu.SemaphoreType.DMA((4, per))]
        + [pltpu.VMEM((rows, cols), f32) for _ in range(3)]
        + [
            pltpu.VMEM((kinds, width, width), f32),
            pltpu.VMEM((width, width), f32),
            pltpu.VMEM((width, width), f32),
            pltpu.SemaphoreType.DMA((6,)),
        ],
        compiler_params=pltpu.CompilerParams(
            collective_id=0, has_side_effects=True, vmem_limit_bytes=60 * 1024 * 1024
        ),
    )(
        order,
        pos,
        step_size,
        block_kind,
        positions.reshape(flat),
        momenta.reshape(flat),
        counts,
        exposure,
        precision_diag,
        kind_blocks,
        vertical_coupling,
        matched_coupling,
    )
    return newx.reshape(positions.shape), newp.reshape(positions.shape)


def solution(mesh):
    return jax.shard_map(
        body,
        mesh=mesh,
        in_specs=(
            P(None, ("groups", "row"), None),
            P(None, ("groups", "row"), None),
            P("groups"),
            P(("groups", "row"), None),
            P(("groups", "row"), None),
            P(("groups", "row"), None),
            P(),
            P(),
            P(),
            P(("groups", "row")),
            P(("groups", "row"), None),
        ),
        out_specs=(P(None, ("groups", "row"), None), P(None, ("groups", "row"), None)),
        check_vma=False,
    )
```
